32 devices in a mesh: seg: 4 (over z), sec: 8 (over y, x, core).
Axes of the slice: x: 2, y: 2, z: 4, core: 2. Of those that a mesh axis runs over, the one named last changes fastest.
Arguments:
- wave_block: bfloat16 [4, 2048, 64, 128], P('seg', 'sec'), may hold values from -6 to 6
- left_envs: bfloat16 [4, 64, 128, 24, 128], P('seg', 'sec'), may hold values from -0.109375 to 0.109375
- next_vectors: bfloat16 [4, 64, 128, 1024], P('seg', 'sec'), may hold values from -6 to 6
- site_weights: float32 [4, 24, 1024], P('seg'), may hold values from 0.5 to 2
- kept_counts: int32 [64], replicated, may hold values from 32 to 128
- slots_before: int32 [64], replicated, may hold values from 0 to 63, as said below
- slots_after: int32 [64], replicated, may hold values from 0 to 63, as said below
Outputs:
- mixed_out: bfloat16 [4, 64, 128, 1024], P('seg', 'sec')
The draws below stay inside these ranges and needn't reach their ends.
Inputs may be any that keep to these rules, and one draw needn't show every extreme that they name: `slots_before`: A permutation of the sectors; device p of sec holds before-slots p * 8 to (p + 1) * 8 - 1. `slots_after`: A permutation of the sectors; device p of sec holds after-slots p * 8 to (p + 1) * 8 - 1. Of the sectors in one device's before-slots, at most 1 lie in any one device's after-slots, and exactly 1 for some pair of devices.
All inputs are finite; a program needn't handle non-finite values.
Results may differ from the reference program's by a relative error of at most 0.0058.
Values may be sent and summed in bfloat16 or wider, within the bound.
A program may use at most 192 MiB of HBM per device.

```python
import math
import jax
import jax.numpy as jnp
from jax import lax

M = 128
KW = 24
SD = 8
CAP = 1
COLS = 1024
NSECT = 64
ROWS = 2048
SEGS = 4
N_SEC = 8


def sector_maps(key):
    before = jax.random.permutation(jax.random.fold_in(key, 11), NSECT).astype(jnp.int32)
    offsets = jax.random.permutation(jax.random.fold_in(key, 12), N_SEC)[:SD // CAP].astype(jnp.int32)
    shifts = jnp.repeat(offsets, CAP)
    devices = jnp.arange(N_SEC, dtype=jnp.int32)
    places = jnp.arange(SD, dtype=jnp.int32)
    source_dev = (devices[:, None] - shifts[None, :]) % N_SEC
    sectors = jnp.take(before, source_dev * SD + places[None, :])
    scores = jax.random.randint(jax.random.fold_in(key, 13), (N_SEC, SD), 0, 1048576) * SD + places[None, :]
    shuffle = jnp.argsort(scores, axis=1, stable=True)
    after = jnp.take_along_axis(sectors, shuffle, axis=1)
    return (before, after.reshape(NSECT).astype(jnp.int32))


def draw_slots_before(key, part):
    return sector_maps(key)[0]


def draw_slots_after(key, part):
    return sector_maps(key)[1]


def plant(result, own_key, least, top_value):
    dims = result.shape
    spot = [jax.random.randint(jax.random.fold_in(own_key, axis), (), 0, dims[axis]) for axis in range(len(dims))]
    result = result.at[tuple(spot)].set(least)
    longest = dims.index(max(dims))
    spot[longest] = (spot[longest] + 1) % dims[longest]
    return result.at[tuple(spot)].set(top_value)


def block_levels(own_key, extent, pieces, smallest, high):
    loudness = 1.0
    for axis_at, parts in pieces:
        heights = jax.random.uniform(jax.random.fold_in(jax.random.fold_in(own_key, 6), axis_at), (parts,), jnp.float32, smallest / len(pieces), high / len(pieces))
        loudness = loudness * jnp.repeat(jnp.exp(heights), extent[axis_at] // parts).reshape((-1,) + (1,) * (len(extent) - 1 - axis_at))
    return loudness


def bell_draw(own_key, extent, deviation, bound, shards=(), held_as=jnp.bfloat16):
    array = deviation * jax.random.normal(own_key, extent, jnp.float32)
    if shards:
        array = array * block_levels(own_key, extent, shards, -0.22, 0.18)
    return jnp.clip(array, -bound, bound).astype(held_as)


def setup_inputs(seed: int = 0) -> dict:
    keys = jax.random.split(jax.random.key(seed), 8)
    wave_block = bell_draw(keys[0], (SEGS, ROWS, NSECT, M), 1.0, 6.0, ((0, 4), (1, 8)))
    left_envs = bell_draw(keys[1], (SEGS, NSECT, M, KW, M), (KW * M) ** -0.5, 0.109375, ((0, 4), (1, 8)))
    next_vectors = bell_draw(keys[2], (SEGS, NSECT, M, COLS), 1.0, 6.0, ((0, 4), (1, 8)))
    site_weights = jnp.clip(jnp.exp(math.log(2.0) - 1.3862944 * jax.random.uniform(keys[3], (SEGS, KW, COLS), jnp.float32) ** block_levels(keys[3], (SEGS, KW, COLS), ((0, 4),), -0.2, 0.2)), 0.5, 2.0)
    kept_counts = plant(jax.random.randint(keys[4], (NSECT,), M // 4, M + 1), jax.random.fold_in(keys[4], 1), M // 4, M).astype(jnp.int32)
    slots_before = draw_slots_before(jax.random.fold_in(keys[7], 71), 0)
    slots_after = draw_slots_after(jax.random.fold_in(keys[7], 71), 0)
    return {"wave_block": wave_block, "left_envs": left_envs, "next_vectors": next_vectors, "site_weights": site_weights, "kept_counts": kept_counts, "slots_before": slots_before, "slots_after": slots_after}


def inverse_of(slots):
    length_of = slots.shape[0]
    indices = jnp.arange(length_of, dtype=jnp.int32)
    return jnp.sum(jnp.where(slots[:, None] == indices[None, :], indices[:, None], 0), axis=0).astype(jnp.int32)

def reference(wave_block, left_envs, next_vectors, site_weights, kept_counts, slots_before, slots_after):
    identity = jnp.eye(M, dtype=jnp.float32)
    channel_zero = (jnp.arange(KW) == 0).astype(jnp.float32)
    boundary = identity[:, None, :] * channel_zero[None, :, None]
    boundary = jnp.broadcast_to(boundary[None], (NSECT, M, KW, M))
    incoming = jnp.concatenate([boundary[None], left_envs[:-1].astype(jnp.float32)], axis=0)
    inv_before = inverse_of(slots_before)
    moved = jnp.take(inv_before, slots_after)
    kept_slots = jnp.take(kept_counts, slots_before)
    keep_mask = (jnp.arange(M)[None, :] < kept_slots[:, None]).astype(jnp.float32)

    def segment(inputs):
        wave, env_in, vectors, weights = inputs
        wide = wave.astype(jnp.float32)
        gram_sum = jnp.einsum('rsa,rsb->sab', wide, wide, precision=lax.Precision.HIGHEST)
        gram_sum = gram_sum / ROWS + 0.1 * identity
        gram_slots = jnp.take(gram_sum, slots_before, axis=0)
        factor = jnp.linalg.cholesky(gram_slots)
        inverse = lax.linalg.triangular_solve(factor, jnp.broadcast_to(identity, gram_slots.shape), left_side=True, lower=True)
        inverse = inverse * keep_mask[:, :, None]
        truncated = jnp.einsum('sab,sbwc,sdc->sawd', inverse, env_in, inverse, precision=lax.Precision.HIGHEST).astype(jnp.bfloat16)
        arranged = jnp.take(truncated, moved, axis=0)

        def sector(pair):
            blocks, block_vec = pair
            scaled = (block_vec.astype(jnp.float32)[None] * weights[:, None, :]).astype(jnp.bfloat16)
            return jnp.einsum('awd,wdc->ac', blocks.astype(jnp.float32), scaled.astype(jnp.float32), precision=lax.Precision.HIGHEST).astype(jnp.bfloat16)
        return lax.map(sector, (arranged, vectors))
    return lax.map(segment, (wave_block, incoming, next_vectors, site_weights))
```

```python
import functools

import jax
import jax.numpy as jnp
from jax import lax
from jax.experimental import pallas as pl
from jax.experimental.pallas import tpu as pltpu
from jax.sharding import PartitionSpec as P

VMEM_BYTES = 48 * 1024 * 1024
PANEL = 8


def ring(value, axis, step):
    count = lax.axis_size(axis)
    return lax.ppermute(value, axis, [(i, (i + step) % count) for i in range(count)])


def inverse_of(slots):
    length_of = slots.shape[0]
    indices = jnp.arange(length_of, dtype=jnp.int32)
    return jnp.sum(jnp.where(slots[:, None] == indices[None, :], indices[:, None], 0), axis=0)


def pick(table, index):
    hits = index[:, None] == jnp.arange(table.shape[0], dtype=jnp.int32)[None, :]
    return jnp.sum(jnp.where(hits, table[None, :], 0), axis=1)


def place_for(owner, devices):
    hits = owner[None, :] == jnp.arange(devices, dtype=jnp.int32)[:, None]
    return jnp.sum(jnp.where(hits, jnp.arange(owner.shape[0], dtype=jnp.int32)[None, :], 0), axis=1)


def gram_kernel(place_ref, wave_ref, out_ref, wide):
    group = wave_ref.shape[1]
    rows = wave_ref.shape[0]
    wide[...] = wave_ref[...].astype(jnp.float32).reshape(wide.shape)
    base = pl.program_id(0) * group
    for s in range(group):
        x = wide[pl.ds(s, rows, stride=group), :].astype(jnp.bfloat16)
        out_ref[place_ref[base + s]] = lax.dot_general(
            x, x, (((0,), (0,)), ((), ())), preferred_element_type=jnp.float32
        )


def grams(wave, place):
    rows, sectors, block = wave.shape
    group = 16
    return pl.pallas_call(
        gram_kernel,
        grid_spec=pltpu.PrefetchScalarGridSpec(
            num_scalar_prefetch=1,
            grid=(sectors // group,),
            in_specs=[pl.BlockSpec((rows, group, block), lambda i, place: (0, i, 0))],
            out_specs=pl.BlockSpec((sectors, block, block), lambda i, place: (0, 0, 0)),
            scratch_shapes=[pltpu.VMEM((rows * group, block), jnp.float32)],
        ),
        out_shape=jax.ShapeDtypeStruct((sectors, block, block), jnp.float32),
        compiler_params=pltpu.CompilerParams(vmem_limit_bytes=VMEM_BYTES),
        cost_estimate=pl.CostEstimate(
            flops=2 * rows * sectors * block * block,
            bytes_accessed=2 * rows * sectors * block + 4 * sectors * block * block,
            transcendentals=0,
        ),
    )(place, wave)


def factor_kernel(total_rows, kept_ref, gram_ref, out_ref, c):
    width, size, _ = gram_ref.shape
    row_at = lax.broadcasted_iota(jnp.int32, (size, size), 0)
    col_at = lax.broadcasted_iota(jnp.int32, (size, size), 1)
    ridge = jnp.where(row_at == col_at, 0.1, 0.0).astype(jnp.float32)
    for s in range(width):
        c[pl.ds(s, size, stride=width), :] = gram_ref[s] * (1.0 / total_rows) + ridge
    lane = lax.broadcasted_iota(jnp.int32, (width, size), 1)

    def spread(row, at):
        return jnp.broadcast_to(row[:, at : at + 1], (width, size))

    for p in range(0, size, PANEL):
        rows = [c[(p + k) * width : (p + k + 1) * width, :] for k in range(PANEL)]
        corner = {
            (k, l): spread(rows[k], p + l) for k in range(PANEL) for l in range(k, PANEL)
        }
        inside = (lane >= p) & (lane < p + PANEL)
        rows = [
            jnp.where(inside, jnp.where(lane == p + k, 1.0, 0.0), rows[k]) for k in range(PANEL)
        ]
        for k in range(PANEL):
            pivot = corner[k, k]
            r = lax.rsqrt(pivot)
            r = r * (1.5 - 0.5 * pivot * r * r)
            rows[k] = rows[k] * r
            m = {l: corner[k, l] * r for l in range(k + 1, PANEL)}
            for l in range(k + 1, PANEL):
                for j in range(l, PANEL):
                    corner[l, j] = corner[l, j] - m[l] * m[j]
                rows[l] = rows[l] - m[l] * rows[k]
        for k in range(PANEL):
            c[(p + k) * width : (p + k + 1) * width, :] = rows[k]
        for i in range(p + PANEL, size):
            row = jnp.where(inside, 0.0, c[i * width : (i + 1) * width, :])
            first = spread(rows[0], i) * rows[0]
            second = spread(rows[1], i) * rows[1]
            for k in range(2, PANEL, 2):
                first += spread(rows[k], i) * rows[k]
                second += spread(rows[k + 1], i) * rows[k + 1]
            c[i * width : (i + 1) * width, :] = row - (first + second)
    for s in range(width):
        full = c[pl.ds(s, size, stride=width), :]
        keep = (col_at <= row_at) & (row_at < kept_ref[s])
        out_ref[s] = jnp.where(keep, full, 0.0).astype(out_ref.dtype)


def low_inverses(gram_sum, kept_here, total_rows):
    width, size, _ = gram_sum.shape
    return pl.pallas_call(
        functools.partial(factor_kernel, total_rows),
        in_specs=[
            pl.BlockSpec(memory_space=pltpu.SMEM),
            pl.BlockSpec(memory_space=pltpu.VMEM),
        ],
        out_specs=pl.BlockSpec(memory_space=pltpu.VMEM),
        out_shape=jax.ShapeDtypeStruct(gram_sum.shape, jnp.bfloat16),
        scratch_shapes=[pltpu.VMEM((size * width, size), jnp.float32)],
        compiler_params=pltpu.CompilerParams(vmem_limit_bytes=VMEM_BYTES),
        cost_estimate=pl.CostEstimate(
            flops=16 * size**3 * width, bytes_accessed=6 * size * size * width, transcendentals=0
        ),
    )(kept_here, gram_sum)


def matvec_kernel(
    channels, edge_ref, src_ref, dst_ref, low_ref, env_ref, vec_ref, weight_ref, out_ref, y, t
):
    low = low_ref[0]
    size = low.shape[0]
    columns = vec_ref.shape[2]

    @pl.when(edge_ref[0] == 0)
    def _():
        y[...] = lax.dot_general(
            env_ref[0], low, (((1,), (1,)), ((), ())), preferred_element_type=jnp.float32
        )

    @pl.when(edge_ref[0] != 0)
    def _():
        y[...] = jnp.zeros_like(y)
        y[pl.ds(0, size, stride=channels), :] = low.astype(jnp.float32).T

    for w in range(channels):
        part = y[pl.ds(w, size, stride=channels), :].astype(jnp.bfloat16)
        t[:, w * size : (w + 1) * size] = jnp.dot(
            low, part, preferred_element_type=jnp.float32
        ).astype(jnp.bfloat16)
    chunk = 256
    for at in range(0, columns, chunk):
        v = vec_ref[0, :, at : at + chunk].astype(jnp.float32)
        total = None
        for w in range(0, channels, 2):
            scaled = jnp.concatenate(
                [
                    (v * weight_ref[w + z : w + z + 1, at : at + chunk]).astype(jnp.bfloat16)
                    for z in range(2)
                ],
                axis=0,
            )
            term = jnp.dot(
                t[:, w * size : (w + 2) * size], scaled, preferred_element_type=jnp.float32
            )
            total = term if total is None else total + term
        out_ref[0, :, at : at + chunk] = total.astype(jnp.bfloat16)


def matvecs(low, env, vectors, weights, edge, src, dst, out_blocks):
    width, size, _ = low.shape
    channels = weights.shape[0]
    columns = weights.shape[1]
    return pl.pallas_call(
        functools.partial(matvec_kernel, channels),
        grid_spec=pltpu.PrefetchScalarGridSpec(
            num_scalar_prefetch=3,
            grid=(width,),
            in_specs=[
                pl.BlockSpec((1, size, size), lambda i, e, s, d: (i, 0, 0)),
                pl.BlockSpec((1, size * channels, size), lambda i, e, s, d: (i, 0, 0)),
                pl.BlockSpec((1, size, columns), lambda i, e, s, d: (s[i], 0, 0)),
                pl.BlockSpec((channels, columns), lambda i, e, s, d: (0, 0)),
            ],
            out_specs=pl.BlockSpec((1, size, columns), lambda i, e, s, d: (d[i], 0, 0)),
            scratch_shapes=[
                pltpu.VMEM((size * channels, size), jnp.float32),
                pltpu.VMEM((size, size * channels), jnp.bfloat16),
            ],
        ),
        out_shape=jax.ShapeDtypeStruct((out_blocks, size, columns), jnp.bfloat16),
        compiler_params=pltpu.CompilerParams(vmem_limit_bytes=VMEM_BYTES),
        cost_estimate=pl.CostEstimate(
            flops=2 * width * size * size * channels * (2 * size + columns),
            bytes_accessed=2 * width * size * (channels * size + 2 * columns),
            transcendentals=0,
        ),
    )(edge, src, dst, low, env, vectors, weights)


def copy_kernel(index_ref, in_ref, out_ref):
    out_ref[...] = in_ref[...]


def take_blocks(values, index):
    _, size, columns = values.shape
    return pl.pallas_call(
        copy_kernel,
        grid_spec=pltpu.PrefetchScalarGridSpec(
            num_scalar_prefetch=1,
            grid=(index.shape[0],),
            in_specs=[pl.BlockSpec((1, size, columns), lambda i, index: (index[i], 0, 0))],
            out_specs=pl.BlockSpec((1, size, columns), lambda i, index: (i, 0, 0)),
        ),
        out_shape=jax.ShapeDtypeStruct((index.shape[0], size, columns), values.dtype),
        cost_estimate=pl.CostEstimate(
            flops=0, bytes_accessed=4 * index.shape[0] * size * columns, transcendentals=0
        ),
    )(index, values)


def on_device(
    wave_block, left_envs, next_vectors, site_weights, kept_counts, slots_before, slots_after
):
    devices = lax.axis_size("sec")
    segments = lax.axis_size("seg")
    myself = lax.axis_index("sec")
    _, width, size, channels, _ = left_envs.shape
    total_rows = wave_block.shape[1] * devices
    inv_before = inverse_of(slots_before)
    inv_after = inverse_of(slots_after)
    mine_before = lax.dynamic_slice_in_dim(slots_before, myself * width, width)
    mine_after = lax.dynamic_slice_in_dim(slots_after, myself * width, width)
    before_owner = pick(inv_before, mine_after) // width
    after_owner = pick(inv_after, mine_before) // width

    gram_sum = lax.psum_scatter(
        grams(wave_block[0], inv_before), "sec", scatter_dimension=0, tiled=True
    )
    packed = take_blocks(next_vectors[0], place_for(before_owner, devices))
    arrived = lax.all_to_all(packed, "sec", split_axis=0, concat_axis=0, tiled=True)
    arrived = ring(arrived, "seg", -1)
    weights = ring(site_weights[0], "seg", -1)
    low = ring(low_inverses(gram_sum, pick(kept_counts, mine_before), total_rows), "seg", -1)
    edge = (lax.axis_index("seg") == segments - 1).astype(jnp.int32).reshape(1)
    env = left_envs[0].reshape(width, size * channels, size)
    result = matvecs(low, env, arrived, weights, edge, after_owner, after_owner, devices)
    result = ring(result, "seg", 1)
    returned = lax.all_to_all(result, "sec", split_axis=0, concat_axis=0, tiled=True)
    return take_blocks(returned, before_owner)[None]


def solution(mesh):
    placed = (
        P("seg", "sec", None, None),
        P("seg", "sec", None, None, None),
        P("seg", "sec", None, None),
        P("seg", None, None),
        P(),
        P(),
        P(),
    )
    return jax.shard_map(
        on_device,
        mesh=mesh,
        in_specs=placed,
        out_specs=P("seg", "sec", None, None),
        check_vma=False,
    )
```

```python
import functools

import jax
import jax.numpy as jnp
from jax import lax
from jax.experimental import pallas as pl
from jax.experimental.pallas import tpu as pltpu
from jax.sharding import PartitionSpec as P

VMEM_BYTES = 48 * 1024 * 1024
PANEL = 8
MESH = pl.DeviceIdType.MESH


def ring(value, axis, step):
    count = lax.axis_size(axis)
    return lax.ppermute(value, axis, [(i, (i + step) % count) for i in range(count)])


def inverse_of(slots):
    length_of = slots.shape[0]
    indices = jnp.arange(length_of, dtype=jnp.int32)
    return jnp.sum(jnp.where(slots[:, None] == indices[None, :], indices[:, None], 0), axis=0)


def pick(table, index):
    hits = index[:, None] == jnp.arange(table.shape[0], dtype=jnp.int32)[None, :]
    return jnp.sum(jnp.where(hits, table[None, :], 0), axis=1)


def place_for(owner, order):
    hits = owner[None, :] == order[:, None]
    return jnp.sum(jnp.where(hits, jnp.arange(owner.shape[0], dtype=jnp.int32)[None, :], 0), axis=1)


def fold(full):
    size = full.shape[0]
    part, half = size // 4, size // 8
    lane = lax.broadcasted_iota(jnp.int32, (part, size), 1)
    second = jnp.where(
        lane < part, pltpu.roll(full[3 * part :], part, 1), full[part : 2 * part]
    )
    third = jnp.where(
        lane[:half] < 2 * part,
        pltpu.roll(full[2 * part + half : 3 * part], 2 * part, 1),
        full[2 * part : 2 * part + half],
    )
    return jnp.concatenate([full[:part], second, third], axis=0)


def unfold(packed, size):
    part, half = size // 4, size // 8
    second, third = packed[part : 2 * part], packed[2 * part : 2 * part + half]
    return jnp.concatenate(
        [
            packed[: 2 * part],
            third,
            pltpu.roll(third, 2 * part, 1),
            pltpu.roll(second, 3 * part, 1),
        ],
        axis=0,
    )


def gram_kernel(
    full, place_ref, env_at, vec_at, wave_ref, env_ref, vec_ref, out_ref, env_out, vec_out, wide, sems
):
    rows, group, size = wave_ref.shape
    places = env_out.shape[0]
    folded = 5 * size // 8
    step = pl.program_id(0)

    def moves():
        for i in range(places):
            yield pltpu.make_async_copy(vec_ref.at[vec_at[i]], vec_out.at[i], sems.at[0, i])
            yield pltpu.make_async_copy(env_ref.at[env_at[i]], env_out.at[i], sems.at[1, i])

    @pl.when(step == 0)
    def _():
        for move in moves():
            move.start()
        if not full:
            out_ref[...] = jnp.zeros_like(out_ref)

    wide[...] = wave_ref[...].astype(jnp.float32).reshape(wide.shape)
    for s in range(group):
        x = wide[pl.ds(s, rows, stride=group), :].astype(jnp.bfloat16)
        gram = lax.dot_general(x, x, (((0,), (0,)), ((), ())), preferred_element_type=jnp.float32)
        out_ref[place_ref[step * group + s]] = fold(gram)

    @pl.when(step == pl.num_programs(0) - 1)
    def _():
        for move in moves():
            move.wait()


def grams_and_moves(wave, env, vectors, place, env_at, vec_at):
    rows, sectors, size = wave.shape
    group = 16
    places = env_at.shape[0]
    folded = 5 * size // 8
    return pl.pallas_call(
        functools.partial(gram_kernel, places * places == sectors),
        grid_spec=pltpu.PrefetchScalarGridSpec(
            num_scalar_prefetch=3,
            grid=(sectors // group,),
            in_specs=[
                pl.BlockSpec((rows, group, size), lambda i, *_: (0, i, 0)),
                pl.BlockSpec(memory_space=pl.ANY),
                pl.BlockSpec(memory_space=pl.ANY),
            ],
            out_specs=[
                pl.BlockSpec((places * places, folded, size), lambda i, *_: (0, 0, 0)),
                pl.BlockSpec(memory_space=pl.ANY),
                pl.BlockSpec(memory_space=pl.ANY),
            ],
            scratch_shapes=[
                pltpu.VMEM((rows * group, size), jnp.float32),
                pltpu.SemaphoreType.DMA((2, places)),
            ],
        ),
        out_shape=[
            jax.ShapeDtypeStruct((places * places, folded, size), jnp.float32),
            jax.ShapeDtypeStruct((places,) + env.shape[1:], env.dtype),
            jax.ShapeDtypeStruct((places,) + vectors.shape[1:], vectors.dtype),
        ],
        compiler_params=pltpu.CompilerParams(vmem_limit_bytes=VMEM_BYTES),
        cost_estimate=pl.CostEstimate(
            flops=2 * rows * sectors * size * size,
            bytes_accessed=2 * rows * sectors * size + 4 * sectors * folded * size,
            transcendentals=0,
        ),
    )(place, env_at, vec_at, wave, env, vectors)


def greet(to_signal, count):
    barrier = pltpu.get_barrier_semaphore()
    for device in to_signal:
        pl.semaphore_signal(barrier, inc=1, device_id=device, device_id_type=MESH)
    pl.semaphore_wait(barrier, count)


def halving_kernel(devices, in_ref, out_ref, total, landed, send_sem, recv_sem):
    me = lax.axis_index("sec")
    segment = lax.axis_index("seg")
    rows = in_ref.shape[1]
    bits = [1 << i for i in range(devices.bit_length() - 1)]

    def partner(bit):
        return (segment, me + bit * (1 - 2 * ((me // bit) % 2)))

    greet([partner(bit) for bit in bits], len(bits))
    orders = [bits, bits[:1] + bits[:0:-1]]
    half = rows // 2
    state = [dict(left=list(range(devices)), used=0) for _ in orders]
    copies = []
    for step in range(len(bits) + 1):
        for h, order in enumerate(orders):
            at = pl.ds(h * half, half)
            now = state[h]
            if step:
                for r, copy, n in now["pending"]:
                    copy.wait_recv()
                    mine = in_ref[r, at, :] if step == 1 else total[r, at, :]
                    if step == len(bits):
                        out_ref[at, :] = mine + landed[h, n]
                    else:
                        total[r, at, :] = mine + landed[h, n]
            if step == len(bits):
                continue
            bit = order[step]
            source = in_ref if step == 0 else total
            keep = [r for r in now["left"] if not r & bit]
            now["pending"] = []
            for i, r in enumerate(keep):
                n = now["used"] + i
                copy = pltpu.make_async_remote_copy(
                    src_ref=source.at[r + bit, at],
                    dst_ref=landed.at[h, n],
                    send_sem=send_sem.at[h, n],
                    recv_sem=recv_sem.at[h, n],
                    device_id=partner(bit),
                    device_id_type=MESH,
                )
                copy.start()
                copies.append(copy)
                now["pending"].append((r, copy, n))
            now["left"] = keep
            now["used"] += len(keep)
    for copy in copies:
        copy.wait_send()


def reduce_scattered(parts):
    devices, rows, size = parts.shape
    return pl.pallas_call(
        functools.partial(halving_kernel, devices),
        in_specs=[pl.BlockSpec(memory_space=pltpu.VMEM)],
        out_specs=pl.BlockSpec(memory_space=pltpu.VMEM),
        out_shape=jax.ShapeDtypeStruct((rows, size), jnp.float32),
        scratch_shapes=[
            pltpu.VMEM(parts.shape, jnp.float32),
            pltpu.VMEM((2, devices - 1, rows // 2, size), jnp.float32),
            pltpu.SemaphoreType.DMA((2, devices - 1)),
            pltpu.SemaphoreType.DMA((2, devices - 1)),
        ],
        compiler_params=pltpu.CompilerParams(
            collective_id=0, has_side_effects=True, vmem_limit_bytes=VMEM_BYTES
        ),
        cost_estimate=pl.CostEstimate(
            flops=devices * rows * size, bytes_accessed=4 * devices * rows * size, transcendentals=0
        ),
    )(parts)


def spread_kernel(
    devices, segments, vec_ref, low_ref, vec_out, low_out, vec_send, vec_recv, low_sems, own_sem
):
    me = lax.axis_index("sec")
    segment = lax.axis_index("seg")
    below = lax.rem(segment + segments - 1, segments)
    above = lax.rem(segment + 1, segments)
    peers = [(segment, lax.rem(me + k, devices)) for k in range(1, devices)]
    greet(peers + [(above, me)], devices)
    low = pltpu.make_async_remote_copy(
        src_ref=low_ref,
        dst_ref=low_out,
        send_sem=low_sems.at[0],
        recv_sem=low_sems.at[1],
        device_id=(below, me),
        device_id_type=MESH,
    )
    low.start()
    copies = []
    for k in range(1, devices):
        copy = pltpu.make_async_remote_copy(
            src_ref=vec_ref.at[k],
            dst_ref=vec_out.at[devices - k],
            send_sem=vec_send.at[k],
            recv_sem=vec_recv.at[devices - k],
            device_id=peers[k - 1],
            device_id_type=MESH,
        )
        copy.start()
        copies.append(copy)
    own = pltpu.make_async_copy(vec_ref.at[0], vec_out.at[0], own_sem)
    own.start()
    own.wait()
    for copy in copies:
        copy.wait()
    low.wait()


def spread_out(vectors, low):
    devices = vectors.shape[0]
    return pl.pallas_call(
        functools.partial(spread_kernel, devices, lax.axis_size("seg")),
        in_specs=[pl.BlockSpec(memory_space=pl.ANY)] * 2,
        out_specs=[pl.BlockSpec(memory_space=pl.ANY)] * 2,
        out_shape=[
            jax.ShapeDtypeStruct(vectors.shape, vectors.dtype),
            jax.ShapeDtypeStruct(low.shape, low.dtype),
        ],
        scratch_shapes=[
            pltpu.SemaphoreType.DMA((devices,)),
            pltpu.SemaphoreType.DMA((devices,)),
            pltpu.SemaphoreType.DMA((2,)),
            pltpu.SemaphoreType.DMA,
        ],
        compiler_params=pltpu.CompilerParams(
            collective_id=1, has_side_effects=True, vmem_limit_bytes=VMEM_BYTES
        ),
        cost_estimate=pl.CostEstimate(
            flops=0, bytes_accessed=4 * vectors.size + 8 * low.size, transcendentals=0
        ),
    )(vectors, low)


def factor_kernel(total_rows, kept_ref, gram_ref, out_ref, c):
    width, size, _ = out_ref.shape
    folded = gram_ref.shape[0] // width
    row_at = lax.broadcasted_iota(jnp.int32, (size, size), 0)
    col_at = lax.broadcasted_iota(jnp.int32, (size, size), 1)
    ridge = jnp.where(row_at == col_at, 0.1, 0.0).astype(jnp.float32)
    for s in range(width):
        c[pl.ds(s, size, stride=width), :] = (
            unfold(gram_ref[s * folded : (s + 1) * folded, :], size) * (1.0 / total_rows) + ridge
        )
    lane = lax.broadcasted_iota(jnp.int32, (width, size), 1)

    def spread(row, at):
        return jnp.broadcast_to(row[:, at : at + 1], (width, size))

    for p in range(0, size, PANEL):
        rows = [c[(p + k) * width : (p + k + 1) * width, :] for k in range(PANEL)]
        corner = {
            (k, l): spread(rows[k], p + l) for k in range(PANEL) for l in range(k, PANEL)
        }
        inside = (lane >= p) & (lane < p + PANEL)
        rows = [
            jnp.where(inside, jnp.where(lane == p + k, 1.0, 0.0), rows[k]) for k in range(PANEL)
        ]
        for k in range(PANEL):
            pivot = corner[k, k]
            r = lax.rsqrt(pivot)
            r = r * (1.5 - 0.5 * pivot * r * r)
            rows[k] = rows[k] * r
            m = {l: corner[k, l] * r for l in range(k + 1, PANEL)}
            for l in range(k + 1, PANEL):
                for j in range(l, PANEL):
                    corner[l, j] = corner[l, j] - m[l] * m[j]
                rows[l] = rows[l] - m[l] * rows[k]
        for k in range(PANEL):
            c[(p + k) * width : (p + k + 1) * width, :] = rows[k]
        for i in range(p + PANEL, size):
            row = jnp.where(inside, 0.0, c[i * width : (i + 1) * width, :])
            first = spread(rows[0], i) * rows[0]
            second = spread(rows[1], i) * rows[1]
            for k in range(2, PANEL, 2):
                first += spread(rows[k], i) * rows[k]
                second += spread(rows[k + 1], i) * rows[k + 1]
            c[i * width : (i + 1) * width, :] = row - (first + second)
    for s in range(width):
        full = c[pl.ds(s, size, stride=width), :]
        keep = (col_at <= row_at) & (row_at < kept_ref[s])
        out_ref[s] = jnp.where(keep, full, 0.0)


def low_inverses(gram_sum, kept_here, total_rows):
    width = kept_here.shape[0]
    size = gram_sum.shape[1]
    return pl.pallas_call(
        functools.partial(factor_kernel, total_rows),
        in_specs=[
            pl.BlockSpec(memory_space=pltpu.SMEM),
            pl.BlockSpec(memory_space=pltpu.VMEM),
        ],
        out_specs=pl.BlockSpec(memory_space=pltpu.VMEM),
        out_shape=jax.ShapeDtypeStruct((width, size, size), jnp.float32),
        scratch_shapes=[pltpu.VMEM((size * width, size), jnp.float32)],
        compiler_params=pltpu.CompilerParams(vmem_limit_bytes=VMEM_BYTES),
        cost_estimate=pl.CostEstimate(
            flops=16 * size**3 * width, bytes_accessed=6 * size * size * width, transcendentals=0
        ),
    )(kept_here, gram_sum)


def split(value):
    high = value.astype(jnp.bfloat16)
    return high, (value - high.astype(jnp.float32)).astype(jnp.bfloat16)


def matvec_kernel(
    devices, segments, low_ref, env_ref, vec_ref, weight_ref, out_ref, y, t, result, send_sem, recv_sem
):
    me = lax.axis_index("sec")
    segment = lax.axis_index("seg")
    below = lax.rem(segment + segments - 1, segments)
    above = lax.rem(segment + 1, segments)
    step = pl.program_id(0)
    channels, columns = weight_ref.shape
    size = low_ref.shape[1]

    def send(k):
        return pltpu.make_async_remote_copy(
            src_ref=result.at[k],
            dst_ref=out_ref.at[lax.rem(devices - k, devices)],
            send_sem=send_sem.at[k],
            recv_sem=recv_sem.at[lax.rem(devices - k, devices)],
            device_id=(above, lax.rem(me + k, devices)),
            device_id_type=MESH,
        )

    @pl.when(step == 0)
    def _():
        greet([(below, lax.rem(me + k, devices)) for k in range(devices)], devices)

    high, low = split(low_ref[0])

    @pl.when(segment != segments - 1)
    def _():
        env = env_ref[0]
        y[...] = lax.dot_general(
            jnp.concatenate([env, env], axis=1),
            jnp.concatenate([high, low], axis=1),
            (((1,), (1,)), ((), ())),
            preferred_element_type=jnp.float32,
        )

    @pl.when(segment == segments - 1)
    def _():
        y[...] = jnp.zeros_like(y)
        y[pl.ds(0, size, stride=channels), :] = low_ref[0].T

    left = jnp.concatenate([high, low, high], axis=1)
    for w in range(0, channels, 2):
        pairs = [split(y[pl.ds(w + z, size, stride=channels), :]) for z in range(2)]
        y_high = jnp.concatenate([pair[0] for pair in pairs], axis=1)
        y_low = jnp.concatenate([pair[1] for pair in pairs], axis=1)
        t[:, w * size : (w + 2) * size] = jnp.dot(
            left,
            jnp.concatenate([y_high, y_high, y_low], axis=0),
            preferred_element_type=jnp.float32,
        ).astype(jnp.bfloat16)
    chunk = 256
    for at in range(0, columns, chunk):
        v = vec_ref[0, :, at : at + chunk].astype(jnp.float32)
        total = None
        for w in range(0, channels, 2):
            scaled = jnp.concatenate(
                [
                    (v * weight_ref[w + z : w + z + 1, at : at + chunk]).astype(jnp.bfloat16)
                    for z in range(2)
                ],
                axis=0,
            )
            term = jnp.dot(
                t[:, w * size : (w + 2) * size], scaled, preferred_element_type=jnp.float32
            )
            total = term if total is None else total + term
        result[step, :, at : at + chunk] = total.astype(jnp.bfloat16)
    send(step).start()

    @pl.when(step == devices - 1)
    def _():
        for k in range(devices):
            send(k).wait()


def matvecs(low, env, vectors, weights):
    devices, size, columns = vectors.shape
    channels = weights.shape[0]
    return pl.pallas_call(
        functools.partial(matvec_kernel, devices, lax.axis_size("seg")),
        grid=(devices,),
        in_specs=[
            pl.BlockSpec((1, size, size), lambda i: (i, 0, 0)),
            pl.BlockSpec((1, size * channels, size), lambda i: (i, 0, 0)),
            pl.BlockSpec((1, size, columns), lambda i: (i, 0, 0)),
            pl.BlockSpec((channels, columns), lambda i: (0, 0)),
        ],
        out_specs=pl.BlockSpec(memory_space=pl.ANY),
        scratch_shapes=[
            pltpu.VMEM((size * channels, size), jnp.float32),
            pltpu.VMEM((size, size * channels), jnp.bfloat16),
            pltpu.VMEM(vectors.shape, jnp.bfloat16),
            pltpu.SemaphoreType.DMA((devices,)),
            pltpu.SemaphoreType.DMA((devices,)),
        ],
        out_shape=jax.ShapeDtypeStruct(vectors.shape, jnp.bfloat16),
        compiler_params=pltpu.CompilerParams(
            collective_id=2, has_side_effects=True, vmem_limit_bytes=VMEM_BYTES
        ),
        cost_estimate=pl.CostEstimate(
            flops=2 * devices * size * size * channels * (2 * size + columns),
            bytes_accessed=2 * devices * size * (channels * size + 2 * columns),
            transcendentals=0,
        ),
    )(low, env, vectors, weights)


def take_kernel(index_ref, in_ref, out_ref, sems):
    moves = [
        pltpu.make_async_copy(in_ref.at[index_ref[i]], out_ref.at[i], sems.at[i])
        for i in range(out_ref.shape[0])
    ]
    for move in moves:
        move.start()
    for move in moves:
        move.wait()


def take_blocks(values, index):
    count = index.shape[0]
    return pl.pallas_call(
        take_kernel,
        in_specs=[
            pl.BlockSpec(memory_space=pltpu.SMEM),
            pl.BlockSpec(memory_space=pl.ANY),
        ],
        out_specs=pl.BlockSpec(memory_space=pl.ANY),
        scratch_shapes=[pltpu.SemaphoreType.DMA((count,))],
        out_shape=jax.ShapeDtypeStruct((count,) + values.shape[1:], values.dtype),
        compiler_params=pltpu.CompilerParams(vmem_limit_bytes=VMEM_BYTES),
        cost_estimate=pl.CostEstimate(
            flops=0, bytes_accessed=4 * count * values[0].size, transcendentals=0
        ),
    )(index, values)


def on_device(
    wave_block, left_envs, next_vectors, site_weights, kept_counts, slots_before, slots_after
):
    devices = lax.axis_size("sec")
    myself = lax.axis_index("sec")
    _, width, size, channels, _ = left_envs.shape
    total_rows = wave_block.shape[1] * devices
    inv_before = inverse_of(slots_before)
    inv_after = inverse_of(slots_after)
    mine_before = lax.dynamic_slice_in_dim(slots_before, myself * width, width)
    mine_after = lax.dynamic_slice_in_dim(slots_after, myself * width, width)
    before_owner = pick(inv_before, mine_after) // width
    after_owner = pick(inv_after, mine_before) // width
    order = lax.rem(myself + jnp.arange(devices, dtype=jnp.int32), devices)
    env_at = place_for(after_owner, order)
    vec_at = place_for(before_owner, order)
    holder, goal = inv_before // width, inv_after // width
    place = (holder ^ myself) * devices + (goal - holder + devices) % devices

    weights = ring(site_weights[0], "seg", -1)
    env = left_envs[0].reshape(width, size * channels, size)
    parts, env, packed = grams_and_moves(
        wave_block[0], env, next_vectors[0], place, env_at, vec_at
    )
    packed = ring(packed, "seg", -1)
    gram_sum = reduce_scattered(parts.reshape(devices, -1, size))
    kept_here = pick(kept_counts, pick(mine_before, env_at))
    low = low_inverses(gram_sum, kept_here, total_rows)
    vectors, low = spread_out(packed, low)
    returned = matvecs(low, env, vectors, weights)
    return take_blocks(returned, (before_owner - myself + devices) % devices)[None]


def solution(mesh):
    placed = (
        P("seg", "sec", None, None),
        P("seg", "sec", None, None, None),
        P("seg", "sec", None, None),
        P("seg", None, None),
        P(),
        P(),
        P(),
    )
    return jax.shard_map(
        on_device,
        mesh=mesh,
        in_specs=placed,
        out_specs=P("seg", "sec", None, None),
        check_vma=False,
    )
```

```python
import functools

import jax
import jax.numpy as jnp
from jax import lax
from jax.experimental import pallas as pl
from jax.experimental.pallas import tpu as pltpu
from jax.sharding import PartitionSpec as P

VMEM_BYTES = 48 * 1024 * 1024
PANEL = 8
MESH = pl.DeviceIdType.MESH


def ring(value, axis, step):
    count = lax.axis_size(axis)
    return lax.ppermute(value, axis, [(i, (i + step) % count) for i in range(count)])


def inverse_of(slots):
    length_of = slots.shape[0]
    indices = jnp.arange(length_of, dtype=jnp.int32)
    return jnp.sum(jnp.where(slots[:, None] == indices[None, :], indices[:, None], 0), axis=0)


def pick(table, index):
    hits = index[:, None] == jnp.arange(table.shape[0], dtype=jnp.int32)[None, :]
    return jnp.sum(jnp.where(hits, table[None, :], 0), axis=1)


def place_for(owner, order):
    hits = owner[None, :] == order[:, None]
    return jnp.sum(jnp.where(hits, jnp.arange(owner.shape[0], dtype=jnp.int32)[None, :], 0), axis=1)


def fold(full):
    size = full.shape[0]
    part, half = size // 4, size // 8
    lane = lax.broadcasted_iota(jnp.int32, (part, size), 1)
    second = jnp.where(
        lane < part, pltpu.roll(full[3 * part :], part, 1), full[part : 2 * part]
    )
    third = jnp.where(
        lane[:half] < 2 * part,
        pltpu.roll(full[2 * part + half : 3 * part], 2 * part, 1),
        full[2 * part : 2 * part + half],
    )
    return jnp.concatenate([full[:part], second, third], axis=0)


def unfold(packed, size):
    part, half = size // 4, size // 8
    second, third = packed[part : 2 * part], packed[2 * part : 2 * part + half]
    return jnp.concatenate(
        [
            packed[: 2 * part],
            third,
            pltpu.roll(third, 2 * part, 1),
            pltpu.roll(second, 3 * part, 1),
        ],
        axis=0,
    )


def gram_kernel(
    full, place_ref, env_at, wave_ref, env_ref, out_ref, env_out, wide, staged, sems
):
    rows, group, size = wave_ref.shape
    places = env_out.shape[0]
    step = pl.program_id(0)
    loads = [
        pltpu.make_async_copy(env_ref.at[env_at[i]], staged.at[i], sems.at[0, i])
        for i in range(places)
    ]
    stores = [
        pltpu.make_async_copy(staged.at[i], env_out.at[i], sems.at[1, i]) for i in range(places)
    ]

    @pl.when(step == 0)
    def _():
        for load in loads:
            load.start()
        if not full:
            out_ref[...] = jnp.zeros_like(out_ref)

    wide[...] = wave_ref[...].astype(jnp.float32).reshape(wide.shape)
    for s in range(group):
        x = wide[pl.ds(s, rows, stride=group), :].astype(jnp.bfloat16)
        gram = lax.dot_general(x, x, (((0,), (0,)), ((), ())), preferred_element_type=jnp.float32)
        out_ref[place_ref[step * group + s]] = fold(gram)

    @pl.when(step == pl.num_programs(0) // 2)
    def _():
        for load, store in zip(loads, stores):
            load.wait()
            store.start()

    @pl.when(step == pl.num_programs(0) - 1)
    def _():
        for store in stores:
            store.wait()


def grams_and_moves(wave, env, place, env_at):
    rows, sectors, size = wave.shape
    group = 16
    places = env_at.shape[0]
    folded = 5 * size // 8
    return pl.pallas_call(
        functools.partial(gram_kernel, places * places == sectors),
        grid_spec=pltpu.PrefetchScalarGridSpec(
            num_scalar_prefetch=2,
            grid=(sectors // group,),
            in_specs=[
                pl.BlockSpec((rows, group, size), lambda i, *_: (0, i, 0)),
                pl.BlockSpec(memory_space=pl.ANY),
            ],
            out_specs=[
                pl.BlockSpec((places * places, folded, size), lambda i, *_: (0, 0, 0)),
                pl.BlockSpec(memory_space=pl.ANY),
            ],
            scratch_shapes=[
                pltpu.VMEM((rows * group, size), jnp.float32),
                pltpu.VMEM((places,) + env.shape[1:], env.dtype),
                pltpu.SemaphoreType.DMA((2, places)),
            ],
        ),
        out_shape=[
            jax.ShapeDtypeStruct((places * places, folded, size), jnp.float32),
            jax.ShapeDtypeStruct((places,) + env.shape[1:], env.dtype),
        ],
        compiler_params=pltpu.CompilerParams(vmem_limit_bytes=VMEM_BYTES),
        cost_estimate=pl.CostEstimate(
            flops=2 * rows * sectors * size * size,
            bytes_accessed=2 * rows * sectors * size + 4 * sectors * folded * size,
            transcendentals=0,
        ),
    )(place, env_at, wave, env)


def greet(to_signal, count):
    barrier = pltpu.get_barrier_semaphore()
    for device in to_signal:
        pl.semaphore_signal(barrier, inc=1, device_id=device, device_id_type=MESH)
    pl.semaphore_wait(barrier, count)


def halving_kernel(devices, in_ref, out_ref, total, landed, send_sem, recv_sem):
    me = lax.axis_index("sec")
    segment = lax.axis_index("seg")
    rows = in_ref.shape[1]
    bits = [1 << i for i in range(devices.bit_length() - 1)]

    def partner(bit):
        return (segment, me + bit * (1 - 2 * ((me // bit) % 2)))

    greet([partner(bit) for bit in bits], len(bits))
    orders = [bits, bits[:1] + bits[:0:-1]]
    half = rows // 2
    state = [dict(left=list(range(devices)), used=0) for _ in orders]
    copies = []
    for step in range(len(bits) + 1):
        for h, order in enumerate(orders):
            at = pl.ds(h * half, half)
            now = state[h]
            if step:
                for r, copy, n in now["pending"]:
                    copy.wait_recv()
                    mine = in_ref[r, at, :] if step == 1 else total[r, at, :]
                    if step == len(bits):
                        out_ref[at, :] = mine + landed[h, n]
                    else:
                        total[r, at, :] = mine + landed[h, n]
            if step == len(bits):
                continue
            bit = order[step]
            source = in_ref if step == 0 else total
            keep = [r for r in now["left"] if not r & bit]
            now["pending"] = []
            for i, r in enumerate(keep):
                n = now["used"] + i
                copy = pltpu.make_async_remote_copy(
                    src_ref=source.at[r + bit, at],
                    dst_ref=landed.at[h, n],
                    send_sem=send_sem.at[h, n],
                    recv_sem=recv_sem.at[h, n],
                    device_id=partner(bit),
                    device_id_type=MESH,
                )
                copy.start()
                copies.append(copy)
                now["pending"].append((r, copy, n))
            now["left"] = keep
            now["used"] += len(keep)
    for copy in copies:
        copy.wait_send()


def reduce_scattered(parts):
    devices, rows, size = parts.shape
    return pl.pallas_call(
        functools.partial(halving_kernel, devices),
        in_specs=[pl.BlockSpec(memory_space=pltpu.VMEM)],
        out_specs=pl.BlockSpec(memory_space=pltpu.VMEM),
        out_shape=jax.ShapeDtypeStruct((rows, size), jnp.float32),
        scratch_shapes=[
            pltpu.VMEM(parts.shape, jnp.float32),
            pltpu.VMEM((2, devices - 1, rows // 2, size), jnp.float32),
            pltpu.SemaphoreType.DMA((2, devices - 1)),
            pltpu.SemaphoreType.DMA((2, devices - 1)),
        ],
        compiler_params=pltpu.CompilerParams(
            collective_id=0, has_side_effects=True, vmem_limit_bytes=VMEM_BYTES
        ),
        cost_estimate=pl.CostEstimate(
            flops=devices * rows * size, bytes_accessed=4 * devices * rows * size, transcendentals=0
        ),
    )(parts)


def factor_kernel(total_rows, kept_ref, gram_ref, out_ref, c):
    width, size, _ = out_ref.shape
    folded = gram_ref.shape[0] // width
    row_at = lax.broadcasted_iota(jnp.int32, (size, size), 0)
    col_at = lax.broadcasted_iota(jnp.int32, (size, size), 1)
    ridge = jnp.where(row_at == col_at, 0.1, 0.0).astype(jnp.float32)
    for s in range(width):
        c[pl.ds(s, size, stride=width), :] = (
            unfold(gram_ref[s * folded : (s + 1) * folded, :], size) * (1.0 / total_rows) + ridge
        )
    lane = lax.broadcasted_iota(jnp.int32, (width, size), 1)

    def spread(row, at):
        return jnp.broadcast_to(row[:, at : at + 1], (width, size))

    for p in range(0, size, PANEL):
        rows = [c[(p + k) * width : (p + k + 1) * width, :] for k in range(PANEL)]
        corner = {
            (k, l): spread(rows[k], p + l) for k in range(PANEL) for l in range(k, PANEL)
        }
        inside = (lane >= p) & (lane < p + PANEL)
        rows = [
            jnp.where(inside, jnp.where(lane == p + k, 1.0, 0.0), rows[k]) for k in range(PANEL)
        ]
        for k in range(PANEL):
            pivot = corner[k, k]
            r = lax.rsqrt(pivot)
            r = r * (1.5 - 0.5 * pivot * r * r)
            rows[k] = rows[k] * r
            m = {l: corner[k, l] * r for l in range(k + 1, PANEL)}
            for l in range(k + 1, PANEL):
                for j in range(l, PANEL):
                    corner[l, j] = corner[l, j] - m[l] * m[j]
                rows[l] = rows[l] - m[l] * rows[k]
        for k in range(PANEL):
            c[(p + k) * width : (p + k + 1) * width, :] = rows[k]
        for i in range(p + PANEL, size):
            row = jnp.where(inside, 0.0, c[i * width : (i + 1) * width, :])
            first = spread(rows[0], i) * rows[0]
            second = spread(rows[1], i) * rows[1]
            for k in range(2, PANEL, 2):
                first += spread(rows[k], i) * rows[k]
                second += spread(rows[k + 1], i) * rows[k + 1]
            c[i * width : (i + 1) * width, :] = row - (first + second)
    for s in range(width):
        full = c[pl.ds(s, size, stride=width), :]
        keep = (col_at <= row_at) & (row_at < kept_ref[s])
        out_ref[s] = jnp.where(keep, full, 0.0)


def low_inverses(gram_sum, kept_here, total_rows):
    width = kept_here.shape[0]
    size = gram_sum.shape[1]
    return pl.pallas_call(
        functools.partial(factor_kernel, total_rows),
        in_specs=[
            pl.BlockSpec(memory_space=pltpu.SMEM),
            pl.BlockSpec(memory_space=pltpu.VMEM),
        ],
        out_specs=pl.BlockSpec(memory_space=pltpu.VMEM),
        out_shape=jax.ShapeDtypeStruct((width, size, size), jnp.float32),
        scratch_shapes=[pltpu.VMEM((size * width, size), jnp.float32)],
        compiler_params=pltpu.CompilerParams(vmem_limit_bytes=VMEM_BYTES),
        cost_estimate=pl.CostEstimate(
            flops=1100 * size**3 * width, bytes_accessed=6 * size * size * width, transcendentals=0
        ),
    )(kept_here, gram_sum)


def split(value):
    high = value.astype(jnp.bfloat16)
    return high, (value - high.astype(jnp.float32)).astype(jnp.bfloat16)


def matvec_kernel(
    devices, segments, low_ref, env_ref, weight_ref, *refs
):
    vec_refs, (out_ref, y, t, vec, result, send_sem, recv_sem) = refs[:devices], refs[devices:]
    me = lax.axis_index("sec")
    segment = lax.axis_index("seg")
    below = lax.rem(segment + segments - 1, segments)
    above = lax.rem(segment + 1, segments)
    step = pl.program_id(0)
    channels, columns = weight_ref.shape
    size = low_ref.shape[1]

    def send(k):
        return pltpu.make_async_remote_copy(
            src_ref=result.at[k],
            dst_ref=out_ref.at[lax.rem(devices - k, devices)],
            send_sem=send_sem.at[k],
            recv_sem=recv_sem.at[lax.rem(devices - k, devices)],
            device_id=(above, lax.rem(me + k, devices)),
            device_id_type=MESH,
        )

    @pl.when(step == 0)
    def _():
        greet([(below, lax.rem(me + k, devices)) for k in range(devices)], devices)

    for k in range(devices):

        @pl.when(step == k)
        def _(k=k):
            vec[...] = vec_refs[k][...]

    high, low = split(low_ref[0])

    @pl.when(segment != segments - 1)
    def _():
        env = env_ref[0]
        y[...] = lax.dot_general(
            jnp.concatenate([env, env], axis=1),
            jnp.concatenate([high, low], axis=1),
            (((1,), (1,)), ((), ())),
            preferred_element_type=jnp.float32,
        )

    @pl.when(segment == segments - 1)
    def _():
        y[...] = jnp.zeros_like(y)
        y[pl.ds(0, size, stride=channels), :] = low_ref[0].T

    left = jnp.concatenate([high, low, high], axis=1)
    for w in range(0, channels, 2):
        pairs = [split(y[pl.ds(w + z, size, stride=channels), :]) for z in range(2)]
        y_high = jnp.concatenate([pair[0] for pair in pairs], axis=1)
        y_low = jnp.concatenate([pair[1] for pair in pairs], axis=1)
        t[:, w * size : (w + 2) * size] = jnp.dot(
            left,
            jnp.concatenate([y_high, y_high, y_low], axis=0),
            preferred_element_type=jnp.float32,
        ).astype(jnp.bfloat16)
    chunk = 256
    for at in range(0, columns, chunk):
        v = vec[:, at : at + chunk].astype(jnp.float32)
        total = None
        for w in range(0, channels, 2):
            scaled = jnp.concatenate(
                [
                    (v * weight_ref[w + z : w + z + 1, at : at + chunk]).astype(jnp.bfloat16)
                    for z in range(2)
                ],
                axis=0,
            )
            term = jnp.dot(
                t[:, w * size : (w + 2) * size], scaled, preferred_element_type=jnp.float32
            )
            total = term if total is None else total + term
        result[step, :, at : at + chunk] = total.astype(jnp.bfloat16)
    send(step).start()

    @pl.when(step == devices - 1)
    def _():
        for k in range(devices):
            send(k).wait()


def matvecs(low, env, vectors, weights):
    devices = len(vectors)
    size, columns = vectors[0].shape
    channels = weights.shape[0]
    return pl.pallas_call(
        functools.partial(matvec_kernel, devices, lax.axis_size("seg")),
        grid=(devices,),
        in_specs=[
            pl.BlockSpec((1, size, size), lambda i: (i, 0, 0)),
            pl.BlockSpec((1, size * channels, size), lambda i: (i, 0, 0)),
            pl.BlockSpec((channels, columns), lambda i: (0, 0)),
        ]
        + [pl.BlockSpec((size, columns), lambda i: (0, 0), pipeline_mode=pl.Buffered(1))] * devices,
        out_specs=pl.BlockSpec(memory_space=pl.ANY),
        scratch_shapes=[
            pltpu.VMEM((size * channels, size), jnp.float32),
            pltpu.VMEM((size, size * channels), jnp.bfloat16),
            pltpu.VMEM((size, columns), jnp.bfloat16),
            pltpu.VMEM((devices, size, columns), jnp.bfloat16),
            pltpu.SemaphoreType.DMA((devices,)),
            pltpu.SemaphoreType.DMA((devices,)),
        ],
        out_shape=jax.ShapeDtypeStruct((devices, size, columns), jnp.bfloat16),
        compiler_params=pltpu.CompilerParams(
            collective_id=1, has_side_effects=True, vmem_limit_bytes=VMEM_BYTES
        ),
        cost_estimate=pl.CostEstimate(
            flops=2 * devices * size * size * channels * (2 * size + columns),
            bytes_accessed=2 * devices * size * (channels * size + 2 * columns),
            transcendentals=0,
        ),
    )(low, env, weights, *vectors)


def take_kernel(index_ref, in_ref, out_ref, sems):
    moves = [
        pltpu.make_async_copy(in_ref.at[index_ref[i]], out_ref.at[i], sems.at[i])
        for i in range(out_ref.shape[0])
    ]
    for move in moves:
        move.start()
    for move in moves:
        move.wait()


def take_blocks(values, index):
    count = index.shape[0]
    return pl.pallas_call(
        take_kernel,
        in_specs=[
            pl.BlockSpec(memory_space=pltpu.SMEM),
            pl.BlockSpec(memory_space=pl.ANY),
        ],
        out_specs=pl.BlockSpec(memory_space=pl.ANY),
        scratch_shapes=[pltpu.SemaphoreType.DMA((count,))],
        out_shape=jax.ShapeDtypeStruct((count,) + values.shape[1:], values.dtype),
        compiler_params=pltpu.CompilerParams(vmem_limit_bytes=VMEM_BYTES),
        cost_estimate=pl.CostEstimate(
            flops=0, bytes_accessed=4 * count * values[0].size, transcendentals=0
        ),
    )(index, values)


def part_kernel(index_ref, in_ref, *refs):
    count = len(refs) - 2
    outs, staged, sems = refs[:count], refs[count], refs[count + 1]
    loads = [
        pltpu.make_async_copy(in_ref.at[index_ref[i]], staged.at[i], sems.at[0, i])
        for i in range(count)
    ]
    stores = [
        pltpu.make_async_copy(staged.at[i], outs[i], sems.at[1, i]) for i in range(count)
    ]
    for load in loads:
        load.start()
    for load, store in zip(loads, stores):
        load.wait()
        store.start()
    for store in stores:
        store.wait()


def parted(values, index):
    count = index.shape[0]
    block = values.shape[1:]
    return pl.pallas_call(
        part_kernel,
        in_specs=[
            pl.BlockSpec(memory_space=pltpu.SMEM),
            pl.BlockSpec(memory_space=pl.ANY),
        ],
        out_specs=[pl.BlockSpec(memory_space=pl.ANY)] * count,
        scratch_shapes=[
            pltpu.VMEM((count,) + block, values.dtype),
            pltpu.SemaphoreType.DMA((2, count)),
        ],
        out_shape=[jax.ShapeDtypeStruct(block, values.dtype)] * count,
        compiler_params=pltpu.CompilerParams(vmem_limit_bytes=VMEM_BYTES),
        cost_estimate=pl.CostEstimate(
            flops=0, bytes_accessed=4 * count * values[0].size, transcendentals=0
        ),
    )(index, values)


def on_device(
    wave_block, left_envs, next_vectors, site_weights, kept_counts, slots_before, slots_after
):
    devices = lax.axis_size("sec")
    myself = lax.axis_index("sec")
    _, width, size, channels, _ = left_envs.shape
    total_rows = wave_block.shape[1] * devices
    inv_before = inverse_of(slots_before)
    inv_after = inverse_of(slots_after)
    mine_before = lax.dynamic_slice_in_dim(slots_before, myself * width, width)
    mine_after = lax.dynamic_slice_in_dim(slots_after, myself * width, width)
    before_owner = pick(inv_before, mine_after) // width
    after_owner = pick(inv_after, mine_before) // width
    order = lax.rem(myself + jnp.arange(devices, dtype=jnp.int32), devices)
    env_at = place_for(after_owner, order)
    back = lax.rem(myself + devices - jnp.arange(devices, dtype=jnp.int32), devices)
    vec_at = place_for(before_owner, back)
    holder, goal = inv_before // width, inv_after // width
    place = (holder ^ myself) * devices + (goal - holder + devices) % devices

    env = left_envs[0].reshape(width, size * channels, size)
    segments = lax.axis_size("seg")
    def sent(block, k):
        pairs = [
            (g * devices + p, (g - 1) % segments * devices + (p - k) % devices)
            for g in range(segments)
            for p in range(devices)
        ]
        return lax.ppermute(block, ("seg", "sec"), pairs)

    blocks = parted(next_vectors[0], vec_at)
    early = 5 * devices // 8
    first = [sent(blocks[k], k) for k in range(early)]
    parts, env = grams_and_moves(wave_block[0], env, place, env_at)
    gram_sum = reduce_scattered(parts.reshape(devices, -1, size))
    gram_sum, first, blocks, weights = lax.optimization_barrier(
        (gram_sum, first, blocks, site_weights[0])
    )
    weights = ring(weights, "seg", -1)
    second = [sent(blocks[k], k) for k in range(early, devices)]
    kept_here = pick(kept_counts, pick(mine_before, env_at))
    low = low_inverses(gram_sum, kept_here, total_rows)
    low, second, weights = lax.optimization_barrier((low, second, weights))
    low = ring(low, "seg", -1)
    vectors = first + second
    returned = matvecs(low, env, vectors, weights)
    return take_blocks(returned, (before_owner - myself + devices) % devices)[None]


def solution(mesh):
    placed = (
        P("seg", "sec", None, None),
        P("seg", "sec", None, None, None),
        P("seg", "sec", None, None),
        P("seg", None, None),
        P(),
        P(),
        P(),
    )
    return jax.shard_map(
        on_device,
        mesh=mesh,
        in_specs=placed,
        out_specs=P("seg", "sec", None, None),
        check_vma=False,
    )
```
